768 devices in a mesh: phase: 3 (over z_hi), dp: 8 (over y), mp: 32 (over x, z_lo, core).
Axes of the slice: x: 4, y: 8, z: 12 (z_hi: 3, z_lo: 4; z = z_hi * 4 + z_lo), core: 2. Of those that a mesh axis runs over, the one named last changes fastest.
Arguments:
- memory: bfloat16 [8, 256, 1024], P('dp', None, 'mp'), may hold values from -6 to 6
- states: bfloat16 [3, 8, 256, 1024], P('phase', 'dp', None, 'mp'), may hold values from -6 to 6
- targets: bfloat16 [3, 8, 256, 1024], P('phase', 'dp', None, 'mp'), may hold values from -6 to 6
- w_query: bfloat16 [3, 1024, 16384], P('phase', None, 'mp'), may hold values from -0.1875 to 0.1875
- w_key: bfloat16 [3, 1024, 16384], P('phase', None, 'mp'), may hold values from -0.1875 to 0.1875
- w_value: bfloat16 [3, 1024, 16384], P('phase', None, 'mp'), may hold values from -0.1875 to 0.1875
- w_out: bfloat16 [3, 16384, 1024], P('phase', 'mp'), may hold values from -0.046875 to 0.046875
- src_ids: int32 [8, 256], P('dp'), may hold values from 0 to 3, never falling along the last dimension, each value on 1 to 128 neighbouring positions
- tgt_ids: int32 [8, 256], P('dp'), may hold values from 0 to 3, never falling along the last dimension, each value on 1 to 128 neighbouring positions
- counts: int32 [8], P('dp'), may hold values from 1 to 256
Outputs:
- cross_out: bfloat16 [3, 8, 256, 1024], P('phase', 'dp', None, 'mp')
- loss: float32 [3], P('phase')
- states_grad: bfloat16 [3, 8, 256, 1024], P('phase', 'dp', None, 'mp')
- memory_grad: bfloat16 [8, 256, 1024], P('dp', None, 'mp')
The draws below stay inside these ranges and needn't reach their ends.
Inputs may be any that keep to these rules, and one draw needn't show every extreme that they name: `src_ids`: both id arrays of a sample hold all segment numbers 0 to 3.
All inputs are finite; a program needn't handle non-finite values.
Results may differ from the reference program's by a relative error of at most 0.013.
The reference program's roundings to bfloat16 on the way count: a program that leaves them out, or rounds other values in their place, can miss the bound.
Values may be sent and summed in bfloat16 or wider, within the bound.
A program may use at most 32 MiB of HBM per device.

```python
import math
import jax
import jax.numpy as jnp
import numpy as np
from jax import lax

D = 1024
HEADS = 128
HEAD = 128
SRC = 256
TGT = 256
INNER = 16384
BATCH = 8
N_PHASE = 3


def draw_states(key, part):
    base = jax.random.normal(jax.random.fold_in(key, 11), (N_PHASE, BATCH, TGT, D), jnp.float32)
    return jnp.clip(base, -6.0, 6.0).astype(jnp.bfloat16)


def place_ends(array, own_key, least, largest):
    shape = array.shape
    spot = [jax.random.randint(jax.random.fold_in(own_key, axis), (), 0, shape[axis]) for axis in range(len(shape))]
    array = array.at[tuple(spot)].set(least)
    longest = shape.index(max(shape))
    spot[longest] = (spot[longest] + 1) % shape[longest]
    return array.at[tuple(spot)].set(largest)


def level_of(stream_key, shape, cuts, low, high):
    gain, own = 1.0, jax.random.fold_in(stream_key, 6)
    for axis_at, parts in cuts:
        steps = jnp.exp(jax.random.uniform(jax.random.fold_in(own, axis_at), (parts,), jnp.float32, low / len(cuts), high / len(cuts)))
        gain = gain * jnp.repeat(steps, shape[axis_at] // parts).reshape([-1 if axis == axis_at else 1 for axis in range(len(shape))])
    return gain


def split_up(count, total, reach, slope):
    loads = [(1 << 20) // math.isqrt(grade ** slope) + 1 for grade in range(2, count + 1)]
    surplus, holding = total - reach - (count - 1), [1] * (count - 1)
    while surplus > 0:
        free = [i for i in range(count - 1) if holding[i] < reach]
        whole, budget = sum([loads[i] for i in free]), surplus
        for i in free:
            extra = min(reach - holding[i], max(1, budget * loads[i] // whole), surplus)
            holding[i] = holding[i] + extra
            surplus = surplus - extra
    return np.array([reach] + holding)


def uneven_parts(key, count, total, most, slope):
    if count == 2:
        one = jax.random.randint(key, (), max(1, total - most), min(most, total - 1) + 1)
        return jnp.stack([one, total - one])
    lengths = jnp.asarray(split_up(count, total, most, slope), jnp.int32)
    pairs = (count - 1) // 2
    source_of, receiver = lengths[1:1 + 2 * pairs:2], lengths[2:2 + 2 * pairs:2]
    slack = jnp.minimum(source_of - 1, most - receiver)
    passed = jax.random.randint(jax.random.fold_in(key, 1), (pairs,), 0, 1 << 20) % (slack + 1)
    lengths = lengths.at[1:1 + 2 * pairs:2].set(source_of - passed).at[2:2 + 2 * pairs:2].set(receiver + passed)
    return lengths[jax.random.permutation(jax.random.fold_in(key, 2), count)]


def centred(rng, shape, scale, limit, split=(), dtype=jnp.bfloat16):
    result = jax.random.normal(rng, shape, jnp.float32) * scale
    if len(split) > 0:
        result = level_of(rng, shape, split, -0.22, 0.18) * result
    return jnp.clip(result, min=-limit, max=limit).astype(dtype)


def setup_inputs(seed: int = 0) -> dict:
    keys = jax.random.split(jax.random.key(seed), 11)
    memory = centred(keys[0], (BATCH, SRC, D), 1.0, 6.0, ((0, 8), (2, 32)))
    states = draw_states(jax.random.fold_in(keys[10], 71), 0)
    targets = centred(keys[2], (N_PHASE, BATCH, TGT, D), 1.0, 6.0, ((0, 3), (1, 8), (3, 32)))
    w_query = centred(keys[3], (N_PHASE, D, INNER), D ** -0.5, 0.1875, ((0, 3), (2, 32)))
    w_key = centred(keys[4], (N_PHASE, D, INNER), D ** -0.5, 0.1875, ((0, 3), (2, 32)))
    w_value = centred(keys[5], (N_PHASE, D, INNER), D ** -0.5, 0.1875, ((0, 3), (2, 32)))
    w_out = centred(keys[6], (N_PHASE, INNER, D), INNER ** -0.5, 0.046875, ((0, 3), (1, 32)))
    src_ids = jax.vmap(lambda own: jnp.searchsorted(jnp.cumsum(uneven_parts(own, 4, SRC, SRC // 2, 1)), jnp.arange(SRC), side="right"))(jax.random.split(keys[7], BATCH)).reshape((BATCH, SRC)).astype(jnp.int32)
    tgt_ids = jax.vmap(lambda own: jnp.searchsorted(jnp.cumsum(uneven_parts(own, 4, TGT, TGT // 2, 1)), jnp.arange(TGT), side="right"))(jax.random.split(keys[8], BATCH)).reshape((BATCH, TGT)).astype(jnp.int32)
    counts = place_ends(jax.random.randint(keys[9], (BATCH,), 1, TGT + 1), jax.random.fold_in(keys[9], 1), 1, TGT).astype(jnp.int32)
    return dict(memory=memory, states=states, targets=targets, w_query=w_query, w_key=w_key, w_value=w_value, w_out=w_out, src_ids=src_ids, tgt_ids=tgt_ids, counts=counts)


def sample_pass(x, mem, tgt, src_id, tgt_id, count, wq, wk, wv, wo):
    q = jnp.dot(x, wq, preferred_element_type=jnp.float32).astype(jnp.bfloat16).reshape(TGT, HEADS, HEAD)
    k = jnp.dot(mem, wk, preferred_element_type=jnp.float32).astype(jnp.bfloat16).reshape(SRC, HEADS, HEAD)
    v = jnp.dot(mem, wv, preferred_element_type=jnp.float32).astype(jnp.bfloat16).reshape(SRC, HEADS, HEAD)
    qf = q.astype(jnp.float32)
    kf = k.astype(jnp.float32)
    vf = v.astype(jnp.float32)
    scores = jnp.einsum('the,jhe->htj', qf, kf)
    allowed = tgt_id[:, None] == src_id[None, :]
    scores = jnp.where(allowed[None], scores, -1e30)
    probs = jax.nn.softmax(scores, axis=-1)
    pb = probs.astype(jnp.bfloat16)
    pbf = pb.astype(jnp.float32)
    attended = jnp.einsum('htj,jhe->the', pbf, vf).astype(jnp.bfloat16).reshape(TGT, HEADS * HEAD)
    out = jnp.dot(attended, wo, preferred_element_type=jnp.float32).astype(jnp.bfloat16)
    valid = (jnp.arange(TGT) < count).astype(jnp.bfloat16)
    grad_out = tgt * valid[:, None]
    part = jnp.sum(out.astype(jnp.float32) * grad_out.astype(jnp.float32))
    grad_att = jnp.dot(grad_out, wo.T, preferred_element_type=jnp.float32).astype(jnp.bfloat16).reshape(TGT, HEADS, HEAD)
    gaf = grad_att.astype(jnp.float32)
    grad_prob = jnp.einsum('the,jhe->htj', gaf, vf)
    inner = jnp.sum(probs * grad_prob, axis=-1, keepdims=True)
    grad_score = (probs * (grad_prob - inner)).astype(jnp.bfloat16).astype(jnp.float32)
    grad_q = jnp.einsum('htj,jhe->the', grad_score, kf).astype(jnp.bfloat16).reshape(TGT, HEADS * HEAD)
    grad_k = jnp.einsum('htj,the->jhe', grad_score, qf).astype(jnp.bfloat16).reshape(SRC, HEADS * HEAD)
    grad_v = jnp.einsum('htj,the->jhe', pbf, gaf).astype(jnp.bfloat16).reshape(SRC, HEADS * HEAD)
    grad_x = jnp.dot(grad_q, wq.T, preferred_element_type=jnp.float32)
    grad_m = jnp.dot(grad_k, wk.T, preferred_element_type=jnp.float32) + jnp.dot(grad_v, wv.T, preferred_element_type=jnp.float32)
    return out, part, grad_x, grad_m


def reference(memory, states, targets, w_query, w_key, w_value, w_out, src_ids, tgt_ids, counts):
    total = jnp.sum(counts.astype(jnp.float32))
    outs = []
    losses = []
    state_grads = []
    mem_grad = jnp.zeros((BATCH, SRC, D), jnp.float32)
    for section in range(N_PHASE):
        def one(items):
            x, mem, tgt, sid, tid, cnt = items
            return sample_pass(x, mem, tgt, sid, tid, cnt, w_query[section], w_key[section], w_value[section], w_out[section])
        out, part, grad_x, grad_m = lax.map(one, (states[section], memory, targets[section], src_ids, tgt_ids, counts))
        outs.append(out)
        losses.append(jnp.sum(part) / total)
        state_grads.append((grad_x / total).astype(jnp.bfloat16))
        mem_grad = mem_grad + grad_m
    return jnp.stack(outs), jnp.stack(losses), jnp.stack(state_grads), (mem_grad / total).astype(jnp.bfloat16)
```

```python
import jax
import jax.numpy as jnp
from jax import lax
from jax.experimental import pallas as pl
from jax.experimental.pallas import tpu as pltpu
from jax.sharding import PartitionSpec as P


BF = jnp.bfloat16
F32 = jnp.float32
MESH = pl.DeviceIdType.MESH
HEADS = 4
HEAD = 128
TOK = 256
NEG = -1e30
M, S, T = 0, 1, 2
OUT, GM, GX = 0, 1, 2


def nn(a, b):
    return lax.dot_general(a, b, (((1,), (0,)), ((), ())), preferred_element_type=F32)


def nt(a, b):
    return lax.dot_general(a, b, (((1,), (1,)), ((), ())), preferred_element_type=F32)


def main_kernel(
    mem_in, st_in, tg_in, wq_in, wk_in, wv_in, wo_in, src_ref, tgt_ref, cnt_ref,
    out_o, gx_o, gm_o, loss_o,
    wq, wk, wv, wo, wot, g, xt, bias,
    q_s, k_s, v_s, kt_s, vt_s, do_s, p_s, pb_s, ot_s, dqt_s, dk_s, dv_s,
    pb_out, po, lc, sx, lx, uo, ub, lz, lp, cs, l0, l1, l2, l3,
    lw, r_a, r_b, r_c, s_ab, s_c, rr_c, rr_x, rr_z, rs_c, rs_x, rs_z, r_p, s_p, r_k, s_k, r_l, s_l,
):
    p = lax.axis_index("phase")
    y = lax.axis_index("dp")
    m = lax.axis_index("mp")
    x, z, c = m // 8, (m // 2) % 4, m % 2
    ring_at = p * 4 + z

    sib = (p, y, x * 8 + z * 2 + (1 - c))

    def dev_x(d):
        return (p, y, ((x + d) % 4) * 8 + z * 2 + c)

    def dev_z(zz):
        return (p, y, x * 8 + zz * 2 + c)

    def dev_ring(d):
        at = (ring_at + d + 12) % 12
        return (at // 4, y, x * 8 + (at % 4) * 2 + c)

    def dev_y(d):
        return (p, (y + d) % 8, m)

    def zx(v):
        return (z, z + 1 - 2 * (z % 2), (z + 2) % 4, 3 - z)[v]

    def send(src, dst, ss, rs, dev):
        pltpu.make_async_remote_copy(
            src_ref=src, dst_ref=dst, send_sem=ss, recv_sem=rs, device_id=dev, device_id_type=MESH
        ).start()

    def wait(ref, sem):
        pltpu.make_async_copy(ref, ref, sem).wait()

    own = x * 4 + z
    loads = [pltpu.make_async_copy(src, g.at[a, c, own], lw.at[a]) for a, src in ((M, mem_in), (S, st_in), (T, tg_in))]
    loads.append(pltpu.make_async_copy(wo_in, wo, lw.at[3]))
    for i, (src, dst) in enumerate(((wk_in, wk), (wv_in, wv), (wq_in, wq))):
        for h in range(2):
            loads.append(pltpu.make_async_copy(src.at[:, h], dst.at[h], lw.at[4 + 2 * i + h]))
    for load in loads:
        load.start()

    barrier = pltpu.get_barrier_semaphore()
    greeted = [sib] + [dev_x(d) for d in (1, 2, 3)] + [dev_y(d) for d in range(1, 8)]
    greeted += [dev_ring(d) for d in (-4, -3, -2, -1, 1, 2, 3, 4)]
    for dev in greeted:
        pl.semaphore_signal(barrier, inc=1, device_id=dev, device_id_type=MESH)

    count = cnt_ref[0]
    src_col = jnp.transpose(jnp.broadcast_to(src_ref[...].astype(F32), (TOK, TOK)))
    bias[...] = jnp.where(src_col == tgt_ref[...].astype(F32), 0.0, NEG)
    cs[y] = jnp.full((8, 128), count.astype(F32))
    loads[3].wait()
    for b in range(8):
        part = jnp.transpose(wo[:, b * 128 : (b + 1) * 128])
        for i in range(4):
            blk = b * 4 + i
            wot[blk % 2, blk // 2] = part[i * 32 : (i + 1) * 32]
    for load in loads[:3] + loads[4:]:
        load.wait()

    pl.semaphore_wait(barrier, len(greeted))

    d2 = 2 - 4 * c

    def blk(a, zz):
        return g.at[a, c, x * 4 + zz]

    def to_x(a, zz):
        for d in (2, 1, 3):
            send(blk(a, zz), blk(a, zz), s_ab.at[a], r_b.at[a, d - 1], dev_x(d))

    def to_z(a):
        for v in (3, 2, 1):
            send(blk(a, z), blk(a, z), s_ab.at[a], r_a.at[a, v - 1], dev_z(zx(v)))

    def to_sib(a, d):
        chunk = g.at[a, c, pl.ds(((x - d + 4) % 4) * 4, 4)]
        send(chunk, chunk, s_c.at[a], r_c.at[a, d], sib)

    def put(a, half, d):
        xx = (x - d + 4) % 4
        rows = g[a, half, pl.ds(xx * 4, 4)].reshape(128, TOK)
        if a == T:
            lane = lax.broadcasted_iota(jnp.int32, (128, TOK), 1)
            rows = jnp.where(lane < count, rows.astype(F32), 0.0).astype(BF)
        col = pl.multiple_of(half * 512 + xx * 128, 128)
        xt[a, :, pl.ds(col, 128)] = jnp.transpose(rows)

    send(blk(M, z), blk(M, z), s_ab.at[M], r_a.at[M, 2], dev_ring(d2))
    send(blk(M, z), blk(M, z), s_ab.at[M], r_a.at[M, 0], dev_ring(1))
    send(blk(M, z), blk(M, z), s_ab.at[M], r_a.at[M, 1], dev_ring(-1))
    to_x(M, z)
    to_z(S)
    to_z(T)
    for d in range(1, 8):
        send(cs.at[y], cs.at[y], s_k.at[0], r_k.at[0], dev_y(d))
    for slot, zz in ((0, (z + 3) % 4), (1, (z + 1) % 4), (2, (z + 2) % 4)):
        wait(blk(M, zz), r_a.at[M, slot])
        to_x(M, zz)
    to_sib(M, 0)
    for a in (S, T):
        to_x(a, z)
        for v in (1, 2, 3):
            wait(blk(a, zx(v)), r_a.at[a, v - 1])
            to_x(a, zx(v))
        to_sib(a, 0)
        put(a - 1, c, 0)

    def arrive(a):
        for d in (1, 3, 2):
            wait(g.at[a, c, pl.ds(((x - d + 4) % 4) * 4, 4)], r_b.at[a, d - 1])
            to_sib(a, d)
            put(a, c, d)

    def arrive_sib(a):
        for d in (0, 1, 3, 2):
            wait(g.at[a, 1 - c, pl.ds(((x - d + 4) % 4) * 4, 4)], r_c.at[a, d])
            put(a, 1 - c, d)

    arrive(M)
    arrive_sib(M)
    k_s[...] = nn(xt[M], wk[...].reshape(1024, 512)).astype(BF)
    v_s[...] = nn(xt[M], wv[...].reshape(1024, 512)).astype(BF)
    kt_s[...] = jnp.transpose(k_s[...])
    vt_s[...] = jnp.transpose(v_s[...])
    arrive(S)
    arrive_sib(S)
    q_s[...] = nn(xt[S], wq[...].reshape(1024, 512)).astype(BF)

    def head(h):
        return slice(h * HEAD, (h + 1) * HEAD)

    for h in range(HEADS):
        scores = nt(k_s[:, head(h)], q_s[:, head(h)]) + bias[...]
        top = jnp.max(scores, axis=0, keepdims=True)
        e = jnp.exp(scores - top)
        probs = e * (1.0 / jnp.sum(e, axis=0, keepdims=True))
        low = probs.astype(BF)
        p_s[h] = probs
        pb_s[h] = low
        ot_s[head(h), :] = nn(vt_s[head(h), :], low).astype(BF)
        if h == 1:
            put(T, c, 0)
            arrive(T)

    orders = {
        OUT: [(zx(v), v - 1, dev_z(zx(v))) for v in (3, 2, 1)],
        GX: [(zx(v), v - 1, dev_z(zx(v))) for v in (3, 2, 1)],
        GM: [((z + 2) % 4, 2, dev_ring(-d2)), ((z + 1) % 4, 0, dev_ring(1)), ((z + 3) % 4, 1, dev_ring(-1))],
    }
    for i in orders:
        orders[i].append((z, 3, None))

    def sum_start(i, part):
        pb_out[i] = part(1 - c).astype(BF).reshape(4, 4, 32, TOK)
        for zz, key, _ in orders[i]:
            send(pb_out.at[i, :, zz], lc.at[i, :, zz], rs_c.at[i], rr_c.at[i, key], sib)
        po[i] = part(c).reshape(4, 4, 32, TOK)

    def sum_x(i):
        for zz, key, _ in orders[i]:
            wait(lc.at[i, :, zz], rr_c.at[i, key])
            total = po[i, :, zz] + lc[i, :, zz].astype(F32)
            po[i, :, zz] = total
            sx[i, :, zz] = total.astype(BF)
            for d in (2, 1, 3):
                send(sx.at[i, (x + d) % 4, zz], lx.at[i, zz, d - 1], rs_x.at[i], rr_x.at[i, key], dev_x(d))

    def sum_z(i):
        for zz, key, dev in orders[i]:
            wait(lx.at[i, zz], rr_x.at[i, key])
            got = lx[i, zz].astype(F32)
            total = po[i, x, zz] + got[0] + got[1] + got[2]
            if dev is None:
                uo[i] = total
            else:
                ub[i, zz] = total.astype(BF)
                send(ub.at[i, zz], lz.at[i, key], rs_z.at[i], rr_z.at[i, key], dev)

    def sum_end(i):
        for key in range(3):
            wait(lz.at[i, key], rr_z.at[i, key])
        got = lz[i].astype(F32)
        return uo[i] + got[0] + got[1] + got[2]

    sum_start(OUT, lambda half: nn(wot[half].reshape(512, 512), ot_s[...]))
    arrive_sib(T)
    do_s[...] = nn(xt[T], wot[...].reshape(1024, 512)).astype(BF)
    sum_x(OUT)

    inner_all = jnp.zeros((1, TOK), F32)
    for h in range(HEADS):
        dprob = nt(v_s[:, head(h)], do_s[:, head(h)])
        probs = p_s[h]
        inner = jnp.sum(probs * dprob, axis=0, keepdims=True)
        inner_all += inner
        ds = (probs * (dprob - inner)).astype(BF)
        dk_s[:, head(h)] = nn(ds, q_s[:, head(h)]).astype(BF)
        dv_s[:, head(h)] = nn(pb_s[h], do_s[:, head(h)]).astype(BF)
        dqt_s[head(h), :] = nn(kt_s[head(h), :], ds).astype(BF)

    def part_gm(half):
        return nt(wk[half].reshape(512, 512), dk_s[...]) + nt(wv[half].reshape(512, 512), dv_s[...])

    sum_start(GM, part_gm)
    sum_start(GX, lambda half: nn(wq[half].reshape(512, 512), dqt_s[...]))

    row = lax.broadcasted_iota(jnp.int32, (8, 128), 0)
    folded = jnp.broadcast_to(inner_all[:, :128] + inner_all[:, 128:], (8, 128))
    l0[c] = jnp.where(row == 0, folded, 0.0)
    send(l0.at[c], l0.at[c], s_l.at[0], r_l.at[0], sib)

    sum_z(OUT)
    sum_x(GM)
    wait(l0.at[1 - c], r_l.at[0])
    l1[x] = l0[0] + l0[1]
    for d in (1, 2, 3):
        send(l1.at[x], l1.at[x], s_l.at[1], r_l.at[1], dev_x(d))
    sum_x(GX)
    wait(l1.at[pl.ds(0, 3)], r_l.at[1])
    l2[z] = (l1[0] + l1[1]) + (l1[2] + l1[3])
    for v in (1, 2, 3):
        send(l2.at[z], l2.at[z], s_l.at[2], r_l.at[2], dev_z(zx(v)))
    sum_z(GM)
    wait(l2.at[pl.ds(0, 3)], r_l.at[2])
    l3[y] = (l2[0] + l2[1]) + (l2[2] + l2[3])
    for d in range(1, 8):
        send(l3.at[y], l3.at[y], s_l.at[3], r_l.at[3], dev_y(d))
    lp[p] = sum_end(GM).astype(BF)
    for d in (-4, 4):
        send(lp.at[p], lp.at[p], s_p.at[0], r_p.at[0], dev_ring(d))
    sum_z(GX)
    out_o[...] = sum_end(OUT).astype(BF)
    wait(cs.at[pl.ds(0, 7)], r_k.at[0])
    tot = jnp.sum(cs[...], axis=0)
    tot_row = tot[0:1, 0:1]
    tot_all = jnp.broadcast_to(tot_row, (32, TOK))
    wait(l3.at[pl.ds(0, 7)], r_l.at[3])
    loss = jnp.sum(jnp.sum(l3[...], axis=0), keepdims=True)
    loss_o[...] = jnp.broadcast_to(loss / tot_row, (8, 128))
    gx_o[...] = (sum_end(GX) / tot_all).astype(BF)
    wait(lp.at[pl.ds(0, 2)], r_p.at[0])
    got = lp[...].astype(F32)
    gm_o[...] = ((got[0] + got[1] + got[2]) / tot_all).astype(BF)

    for a in range(3):
        wait(g.at[a, 0, pl.ds(0, 15)], s_ab.at[a])
        wait(g.at[a, 0], s_c.at[a])
        wait(pb_out.at[a], rs_c.at[a])
        wait(sx.at[a, pl.ds(0, 3)], rs_x.at[a])
        wait(ub.at[a, pl.ds(0, 3)], rs_z.at[a])
    wait(lp.at[pl.ds(0, 2)], s_p.at[0])
    wait(cs.at[pl.ds(0, 7)], s_k.at[0])
    wait(l0.at[0], s_l.at[0])
    wait(l1.at[pl.ds(0, 3)], s_l.at[1])
    wait(l2.at[pl.ds(0, 3)], s_l.at[2])
    wait(l3.at[pl.ds(0, 7)], s_l.at[3])


def place_kernel(out_i, gx_i, gm_i, loss_i, out_o, gx_o, gm_o, loss_o):
    out_o[...] = out_i[...]
    gx_o[...] = gx_i[...]
    gm_o[...] = gm_i[...]
    loss_o[0] = loss_i[0, 0]


def local(memory, states, targets, w_query, w_key, w_value, w_out, src_ids, tgt_ids, counts):
    vmem = pl.BlockSpec(memory_space=pltpu.VMEM)
    smem = pl.BlockSpec(memory_space=pltpu.SMEM)
    hbm = pl.BlockSpec(memory_space=pl.ANY)
    dma = pltpu.SemaphoreType.DMA
    block = jax.ShapeDtypeStruct((32, TOK), BF)
    split = (16, 2, 32, 512)

    def v(shape, dtype=BF):
        return pltpu.VMEM(shape, dtype)

    results = pl.pallas_call(
        main_kernel,
        out_shape=(block, block, block, jax.ShapeDtypeStruct((8, 128), F32)),
        in_specs=[hbm] * 7 + [vmem, vmem, smem],
        out_specs=[vmem] * 4,
        scratch_shapes=[
            v((2, 16, 32, 512)), v((2, 16, 32, 512)), v((2, 16, 32, 512)), v((512, 1024)), v((2, 16, 32, 512)),
            v((3, 2, 16, 32, TOK)), v((3, TOK, 1024)), v((TOK, TOK), F32),
            v((TOK, 512)), v((TOK, 512)), v((TOK, 512)), v((512, TOK)), v((512, TOK)), v((TOK, 512)),
            v((HEADS, TOK, TOK), F32), v((HEADS, TOK, TOK)), v((512, TOK)), v((512, TOK)), v((TOK, 512)), v((TOK, 512)),
            v((3, 4, 4, 32, TOK)), v((3, 4, 4, 32, TOK), F32), v((3, 4, 4, 32, TOK)), v((3, 4, 4, 32, TOK)),
            v((3, 4, 3, 32, TOK)), v((3, 32, TOK), F32), v((3, 4, 32, TOK)), v((3, 3, 32, TOK)), v((3, 32, TOK)),
            v((8, 8, 128), F32), v((2, 8, 128), F32), v((4, 8, 128), F32), v((4, 8, 128), F32), v((8, 8, 128), F32),
            dma((10,)), dma((3, 3)), dma((3, 3)), dma((3, 4)), dma((3,)), dma((3,)),
            dma((3, 4)), dma((3, 4)), dma((3, 3)), dma((3,)), dma((3,)), dma((3,)),
            dma((1,)), dma((1,)), dma((1,)), dma((1,)), dma((4,)), dma((4,)),
        ],
        compiler_params=pltpu.CompilerParams(
            collective_id=0, has_side_effects=True, vmem_limit_bytes=50 * 1024 * 1024
        ),
        name="cross_attention",
    )(
        memory[0].T, states[0, 0].T, targets[0, 0].T,
        w_query.reshape(split), w_key.reshape(split), w_value.reshape(split), w_out[0],
        src_ids, tgt_ids, counts,
    )
    out, gx, gm, loss = pl.pallas_call(
        place_kernel,
        out_shape=(block, block, block, jax.ShapeDtypeStruct((1,), F32)),
        in_specs=[vmem] * 4,
        out_specs=[vmem, vmem, vmem, smem],
        name="place_outputs",
    )(*results)
    return out.T[None, None], loss, gx.T[None, None], gm.T[None]


def solution(mesh):
    placed = (
        P("dp", None, "mp"),
        P("phase", "dp", None, "mp"),
        P("phase", "dp", None, "mp"),
        P("phase", None, "mp"),
        P("phase", None, "mp"),
        P("phase", None, "mp"),
        P("phase", "mp", None),
        P("dp", None),
        P("dp", None),
        P("dp"),
    )
    return jax.shard_map(
        local,
        mesh=mesh,
        in_specs=placed,
        out_specs=(
            P("phase", "dp", None, "mp"),
            P("phase"),
            P("phase", "dp", None, "mp"),
            P("dp", None, "mp"),
        ),
        check_vma=False,
    )
```

```python
import jax
import jax.numpy as jnp
from jax import lax
from jax.experimental import pallas as pl
from jax.experimental.pallas import tpu as pltpu
from jax.sharding import PartitionSpec as P


BF = jnp.bfloat16
F32 = jnp.float32
MESH = pl.DeviceIdType.MESH
HEADS = 4
HEAD = 128
TOK = 256
NEG = -1e30
M, S, T = 0, 1, 2
OUT, GM, GX = 0, 1, 2


def nn(a, b):
    return lax.dot_general(a, b, (((1,), (0,)), ((), ())), preferred_element_type=F32)


def nt(a, b):
    return lax.dot_general(a, b, (((1,), (1,)), ((), ())), preferred_element_type=F32)


def main_kernel(
    mem_in, st_in, tg_in, wq_in, wk_in, wv_in, wo_in, src_in, tgt_in, cnt_ref,
    out_o, gx_o, gm_o, loss_o,
    wq, wk, wv, wo, wot, g, xt, bias, src_ref, tgt_ref,
    q_s, k_s, v_s, kt_s, vt_s, do_s, p_s, pb_s, ds_s, ot_s, dqt_s, dk_s, dv_s,
    pb_out, po, lc, sx, lx, uo, ub, lz, lp, cs, l0, l1, l2, l3,
    lw, r_a, r_b, r_c, s_ab, s_c, rr_c, rr_x, rr_z, rs_c, rs_x, rs_z, r_p, s_p, r_k, s_k, r_l, s_l,
):
    p = lax.axis_index("phase")
    y = lax.axis_index("dp")
    m = lax.axis_index("mp")
    x, z, c = m // 8, (m // 2) % 4, m % 2
    ring_at = p * 4 + z

    sib = (p, y, x * 8 + z * 2 + (1 - c))

    def dev_x(d):
        return (p, y, ((x + d) % 4) * 8 + z * 2 + c)

    def dev_z(zz):
        return (p, y, x * 8 + zz * 2 + c)

    def dev_ring(d):
        at = (ring_at + d + 12) % 12
        return (at // 4, y, x * 8 + (at % 4) * 2 + c)

    def dev_y(d):
        return (p, (y + d) % 8, m)

    def zx(v):
        return (z, z + 1 - 2 * (z % 2), (z + 2) % 4, 3 - z)[v]

    def send(src, dst, ss, rs, dev):
        pltpu.make_async_remote_copy(
            src_ref=src, dst_ref=dst, send_sem=ss, recv_sem=rs, device_id=dev, device_id_type=MESH
        ).start()

    def wait(ref, sem):
        pltpu.make_async_copy(ref, ref, sem).wait()

    own = x * 4 + z
    loads = [pltpu.make_async_copy(src, g.at[a, c, own], lw.at[a]) for a, src in ((M, mem_in), (S, st_in), (T, tg_in))]
    loads.append(pltpu.make_async_copy(wo_in, wo, lw.at[3]))
    for i, (src, dst) in enumerate(((wk_in, wk), (wv_in, wv), (wq_in, wq))):
        for h in range(2):
            loads.append(pltpu.make_async_copy(src.at[:, h], dst.at[h], lw.at[4 + 2 * i + h]))
    ids = [pltpu.make_async_copy(src, dst, lw.at[10 + i]) for i, (src, dst) in enumerate(((src_in, src_ref), (tgt_in, tgt_ref)))]
    for load in loads + ids:
        load.start()

    barrier = pltpu.get_barrier_semaphore()
    greeted = [sib] + [dev_x(d) for d in (1, 2, 3)] + [dev_y(d) for d in range(1, 8)]
    greeted += [dev_ring(d) for d in (-4, -3, -2, -1, 1, 2, 3, 4)]
    for dev in greeted:
        pl.semaphore_signal(barrier, inc=1, device_id=dev, device_id_type=MESH)

    count = cnt_ref[0]
    cs[y] = jnp.full((8, 128), count.astype(F32))
    for load in loads[:3]:
        load.wait()
    pl.semaphore_wait(barrier, len(greeted))

    d2 = 2 - 4 * c

    def blk(a, zz):
        return g.at[a, c, x * 4 + zz]

    def to_x(a, zz):
        for d in (2, 1, 3):
            send(blk(a, zz), blk(a, zz), s_ab.at[a], r_b.at[a, d - 1], dev_x(d))

    def to_z(a):
        for v in (3, 2, 1):
            send(blk(a, z), blk(a, z), s_ab.at[a], r_a.at[a, v - 1], dev_z(zx(v)))

    def to_sib(a, d):
        chunk = g.at[a, c, pl.ds(((x - d + 4) % 4) * 4, 4)]
        send(chunk, chunk, s_c.at[a], r_c.at[a, d], sib)

    def put(a, half, d):
        xx = (x - d + 4) % 4
        rows = g[a, half, pl.ds(xx * 4, 4)].reshape(128, TOK)
        if a == T:
            lane = lax.broadcasted_iota(jnp.int32, (128, TOK), 1)
            rows = jnp.where(lane < count, rows.astype(F32), 0.0).astype(BF)
        col = pl.multiple_of(half * 512 + xx * 128, 128)
        xt[a, :, pl.ds(col, 128)] = jnp.transpose(rows)

    send(blk(M, z), blk(M, z), s_ab.at[M], r_a.at[M, 2], dev_ring(d2))
    send(blk(M, z), blk(M, z), s_ab.at[M], r_a.at[M, 0], dev_ring(1))
    send(blk(M, z), blk(M, z), s_ab.at[M], r_a.at[M, 1], dev_ring(-1))
    to_x(M, z)
    to_z(S)
    to_z(T)
    for d in range(1, 8):
        send(cs.at[y], cs.at[y], s_k.at[0], r_k.at[0], dev_y(d))

    for load in ids:
        load.wait()
    src_col = jnp.transpose(jnp.broadcast_to(src_ref[...].astype(F32), (TOK, TOK)))
    bias[...] = jnp.where(src_col == tgt_ref[...].astype(F32), 0.0, NEG)
    loads[3].wait()
    for b in range(8):
        part = jnp.transpose(wo[:, b * 128 : (b + 1) * 128])
        for i in range(4):
            at = b * 4 + i
            wot[at % 2, at // 2] = part[i * 32 : (i + 1) * 32]

    for slot, zz in ((0, (z + 3) % 4), (1, (z + 1) % 4), (2, (z + 2) % 4)):
        wait(blk(M, zz), r_a.at[M, slot])
        to_x(M, zz)
    to_sib(M, 0)
    for a in (S, T):
        to_x(a, z)
        for v in (1, 2, 3):
            wait(blk(a, zx(v)), r_a.at[a, v - 1])
            to_x(a, zx(v))
        to_sib(a, 0)
        put(a - 1, c, 0)

    def arrive(a):
        for d in (1, 3, 2):
            wait(g.at[a, c, pl.ds(((x - d + 4) % 4) * 4, 4)], r_b.at[a, d - 1])
            to_sib(a, d)
            put(a, c, d)

    def arrive_sib(a):
        for d in (0, 1, 3, 2):
            wait(g.at[a, 1 - c, pl.ds(((x - d + 4) % 4) * 4, 4)], r_c.at[a, d])
            put(a, 1 - c, d)

    arrive(M)
    arrive_sib(M)
    for load in loads[4:]:
        load.wait()
    k_s[...] = nn(xt[M], wk[...].reshape(1024, 512)).astype(BF)
    v_s[...] = nn(xt[M], wv[...].reshape(1024, 512)).astype(BF)
    kt_s[...] = jnp.transpose(k_s[...])
    vt_s[...] = jnp.transpose(v_s[...])
    arrive(S)
    arrive_sib(S)
    q_s[...] = nn(xt[S], wq[...].reshape(1024, 512)).astype(BF)

    def head(h):
        return slice(h * HEAD, (h + 1) * HEAD)

    for h in range(HEADS):
        scores = nt(k_s[:, head(h)], q_s[:, head(h)]) + bias[...]
        top = jnp.max(scores, axis=0, keepdims=True)
        e = jnp.exp(scores - top)
        probs = e * (1.0 / jnp.sum(e, axis=0, keepdims=True))
        low = probs.astype(BF)
        p_s[h] = probs
        pb_s[h] = low
        ot_s[head(h), :] = nn(vt_s[head(h), :], low).astype(BF)
        if h == 1:
            put(T, c, 0)
            arrive(T)

    along_z = [(zx(v), v - 1, dev_z(zx(v))) for v in (3, 2, 1)] + [(z, 3, None)]
    along_ring = [((z + 2) % 4, 2, dev_ring(-d2)), ((z + 1) % 4, 0, dev_ring(1)), ((z + 3) % 4, 1, dev_ring(-1))]
    along_x = [((x + d) % 4, d - 1, dev_x(d)) for d in (2, 1, 3)] + [(x, 3, None)]

    def chunk(i, buf, at):
        return buf.at[i, at] if i == GM else buf.at[i, :, at]

    def sum_start(i, part):
        pb_out[i] = part(1 - c).astype(BF).reshape(4, 4, 32, TOK)
        for at, key, _ in along_x if i == GM else along_z:
            send(chunk(i, pb_out, at), chunk(i, lc, at), rs_c.at[i], rr_c.at[i, key], sib)
        po[i] = part(c).reshape(4, 4, 32, TOK)

    def sum_first(i):
        for at, key, _ in along_x if i == GM else along_z:
            wait(chunk(i, lc, at), rr_c.at[i, key])
            if i == GM:
                total = po[i, at] + lc[i, at].astype(F32)
                po[i, at] = total
                sx[i, at] = total.astype(BF)
                for zz, slot, dev in along_ring:
                    send(sx.at[i, at, zz], lx.at[i, at, slot], rs_x.at[i], rr_x.at[i, key], dev)
            else:
                total = po[i, :, at] + lc[i, :, at].astype(F32)
                po[i, :, at] = total
                sx[i, :, at] = total.astype(BF)
                for xx, slot, dev in along_x[:3]:
                    send(sx.at[i, xx, at], lx.at[i, at, slot], rs_x.at[i], rr_x.at[i, key], dev)

    def sum_second(i):
        for at, key, dev in along_x if i == GM else along_z:
            wait(lx.at[i, at], rr_x.at[i, key])
            got = lx[i, at].astype(F32)
            total = (po[i, at, z] if i == GM else po[i, x, at]) + got[0] + got[1] + got[2]
            if dev is None:
                uo[i] = total
            else:
                ub[i, at] = total.astype(BF)
                send(ub.at[i, at], lz.at[i, key], rs_z.at[i], rr_z.at[i, key], dev)

    def sum_end(i):
        for key in range(3):
            wait(lz.at[i, key], rr_z.at[i, key])
        got = lz[i].astype(F32)
        return uo[i] + got[0] + got[1] + got[2]

    sum_start(OUT, lambda half: nn(wot[half].reshape(512, 512), ot_s[...]))
    arrive_sib(T)
    do_s[...] = nn(xt[T], wot[...].reshape(1024, 512)).astype(BF)
    sum_first(OUT)

    inner_all = jnp.zeros((1, TOK), F32)
    for h in range(HEADS):
        dprob = nt(v_s[:, head(h)], do_s[:, head(h)])
        probs = p_s[h]
        inner = jnp.sum(probs * dprob, axis=0, keepdims=True)
        inner_all += inner
        ds_s[h] = (probs * (dprob - inner)).astype(BF)
    row = lax.broadcasted_iota(jnp.int32, (8, 128), 0)
    folded = jnp.broadcast_to(inner_all[:, :128] + inner_all[:, 128:], (8, 128))
    l3[y] = jnp.where(row == 0, folded, 0.0)
    for d in range(1, 8):
        send(l3.at[y], l3.at[y], s_l.at[3], r_l.at[3], dev_y(d))
    for h in range(HEADS):
        ds = ds_s[h]
        dk_s[:, head(h)] = nn(ds, q_s[:, head(h)]).astype(BF)
        dv_s[:, head(h)] = nn(pb_s[h], do_s[:, head(h)]).astype(BF)
        dqt_s[head(h), :] = nn(kt_s[head(h), :], ds).astype(BF)

    def part_gm(half):
        return nt(wk[half].reshape(512, 512), dk_s[...]) + nt(wv[half].reshape(512, 512), dv_s[...])

    sum_start(GM, part_gm)
    sum_start(GX, lambda half: nn(wq[half].reshape(512, 512), dqt_s[...]))

    sum_first(GM)
    sum_first(GX)
    sum_second(OUT)
    wait(l3.at[pl.ds(0, 7)], r_l.at[3])
    l0[c] = jnp.sum(l3[...], axis=0)
    send(l0.at[c], l0.at[c], s_l.at[0], r_l.at[0], sib)
    sum_second(GM)
    wait(l0.at[1 - c], r_l.at[0])
    l1[x] = l0[0] + l0[1]
    for d in (1, 2, 3):
        send(l1.at[x], l1.at[x], s_l.at[1], r_l.at[1], dev_x(d))
    lp[p] = sum_end(GM).astype(BF)
    for d in (-4, 4):
        send(lp.at[p], lp.at[p], s_p.at[0], r_p.at[0], dev_ring(d))
    wait(l1.at[pl.ds(0, 3)], r_l.at[1])
    l2[z] = (l1[0] + l1[1]) + (l1[2] + l1[3])
    for v in (1, 2, 3):
        send(l2.at[z], l2.at[z], s_l.at[2], r_l.at[2], dev_z(zx(v)))
    sum_second(GX)
    out_o[...] = sum_end(OUT).astype(BF)
    wait(cs.at[pl.ds(0, 7)], r_k.at[0])
    tot = jnp.sum(cs[...], axis=0)
    tot_row = tot[0:1, 0:1]
    tot_all = jnp.broadcast_to(tot_row, (32, TOK))
    wait(l2.at[pl.ds(0, 3)], r_l.at[2])
    loss = jnp.sum((l2[0] + l2[1]) + (l2[2] + l2[3]), keepdims=True)
    loss_o[...] = jnp.broadcast_to(loss / tot_row, (8, 128))
    gx_o[...] = (sum_end(GX) / tot_all).astype(BF)
    wait(lp.at[pl.ds(0, 2)], r_p.at[0])
    got = lp[...].astype(F32)
    gm_o[...] = ((got[0] + got[1] + got[2]) / tot_all).astype(BF)

    for a in range(3):
        wait(g.at[a, 0, pl.ds(0, 15)], s_ab.at[a])
        wait(g.at[a, 0], s_c.at[a])
        wait(pb_out.at[a], rs_c.at[a])
        wait(sx.at[a, pl.ds(0, 3)], rs_x.at[a])
        wait(ub.at[a, pl.ds(0, 3)], rs_z.at[a])
    wait(lp.at[pl.ds(0, 2)], s_p.at[0])
    wait(cs.at[pl.ds(0, 7)], s_k.at[0])
    wait(l0.at[0], s_l.at[0])
    wait(l1.at[pl.ds(0, 3)], s_l.at[1])
    wait(l2.at[pl.ds(0, 3)], s_l.at[2])
    wait(l3.at[pl.ds(0, 7)], s_l.at[3])


def place_kernel(out_i, gx_i, gm_i, loss_i, out_o, gx_o, gm_o, loss_o):
    out_o[...] = out_i[...]
    gx_o[...] = gx_i[...]
    gm_o[...] = gm_i[...]
    loss_o[0] = loss_i[0, 0]


def local(memory, states, targets, w_query, w_key, w_value, w_out, src_ids, tgt_ids, counts):
    vmem = pl.BlockSpec(memory_space=pltpu.VMEM)
    smem = pl.BlockSpec(memory_space=pltpu.SMEM)
    hbm = pl.BlockSpec(memory_space=pl.ANY)
    dma = pltpu.SemaphoreType.DMA
    block = jax.ShapeDtypeStruct((32, TOK), BF)
    split = (16, 2, 32, 512)

    def v(shape, dtype=BF):
        return pltpu.VMEM(shape, dtype)

    results = pl.pallas_call(
        main_kernel,
        out_shape=(block, block, block, jax.ShapeDtypeStruct((8, 128), F32)),
        in_specs=[hbm] * 9 + [smem],
        out_specs=[vmem] * 4,
        scratch_shapes=[
            v((2, 16, 32, 512)), v((2, 16, 32, 512)), v((2, 16, 32, 512)), v((512, 1024)), v((2, 16, 32, 512)),
            v((3, 2, 16, 32, TOK)), v((3, TOK, 1024)), v((TOK, TOK), F32),
            v((1, TOK), jnp.int32), v((1, TOK), jnp.int32),
            v((TOK, 512)), v((TOK, 512)), v((TOK, 512)), v((512, TOK)), v((512, TOK)), v((TOK, 512)),
            v((HEADS, TOK, TOK), F32), v((HEADS, TOK, TOK)), v((HEADS, TOK, TOK)), v((512, TOK)), v((512, TOK)), v((TOK, 512)), v((TOK, 512)),
            v((3, 4, 4, 32, TOK)), v((3, 4, 4, 32, TOK), F32), v((3, 4, 4, 32, TOK)), v((3, 4, 4, 32, TOK)),
            v((3, 4, 3, 32, TOK)), v((3, 32, TOK), F32), v((3, 4, 32, TOK)), v((3, 3, 32, TOK)), v((3, 32, TOK)),
            v((8, 8, 128), F32), v((2, 8, 128), F32), v((4, 8, 128), F32), v((4, 8, 128), F32), v((8, 8, 128), F32),
            dma((12,)), dma((3, 3)), dma((3, 3)), dma((3, 4)), dma((3,)), dma((3,)),
            dma((3, 4)), dma((3, 4)), dma((3, 3)), dma((3,)), dma((3,)), dma((3,)),
            dma((1,)), dma((1,)), dma((1,)), dma((1,)), dma((4,)), dma((4,)),
        ],
        compiler_params=pltpu.CompilerParams(
            collective_id=0, has_side_effects=True, vmem_limit_bytes=62 * 1024 * 1024
        ),
        name="cross_attention",
    )(
        memory[0].T, states[0, 0].T, targets[0, 0].T,
        w_query.reshape(split), w_key.reshape(split), w_value.reshape(split), w_out[0],
        src_ids, tgt_ids, counts,
    )
    out, gx, gm, loss = pl.pallas_call(
        place_kernel,
        out_shape=(block, block, block, jax.ShapeDtypeStruct((1,), F32)),
        in_specs=[vmem, vmem, vmem, smem],
        out_specs=[vmem, vmem, vmem, smem],
        name="place_outputs",
    )(*results)
    return out.T[None, None], loss, gx.T[None, None], gm.T[None]


def solution(mesh):
    placed = (
        P("dp", None, "mp"),
        P("phase", "dp", None, "mp"),
        P("phase", "dp", None, "mp"),
        P("phase", None, "mp"),
        P("phase", None, "mp"),
        P("phase", None, "mp"),
        P("phase", "mp", None),
        P("dp", None),
        P("dp", None),
        P("dp"),
    )
    return jax.shard_map(
        local,
        mesh=mesh,
        in_specs=placed,
        out_specs=(
            P("phase", "dp", None, "mp"),
            P("phase"),
            P("phase", "dp", None, "mp"),
            P("dp", None, "mp"),
        ),
        check_vma=False,
    )
```

```python
import jax
import jax.numpy as jnp
from jax import lax
from jax.experimental import pallas as pl
from jax.experimental.pallas import tpu as pltpu
from jax.sharding import PartitionSpec as P


BF = jnp.bfloat16
F32 = jnp.float32
MESH = pl.DeviceIdType.MESH
HEADS = 4
HEAD = 128
TOK = 256
NEG = -1e30
M, S, T = 0, 1, 2
OUT, GM, GX = 0, 1, 2


def nn(a, b):
    return lax.dot_general(a, b, (((1,), (0,)), ((), ())), preferred_element_type=F32)


def nt(a, b):
    return lax.dot_general(a, b, (((1,), (1,)), ((), ())), preferred_element_type=F32)


def main_kernel(
    mem_in, st_in, tg_in, wq_in, wk_in, wv_in, wo_in, src_in, tgt_in, cnt_ref,
    out_o, gx_o, gm_o, loss_o,
    wq, wk, wv, wo, wot, g, xt, bias, src_ref, tgt_ref,
    q_s, k_s, v_s, kt_s, vt_s, do_s, p_s, pb_s, ds_s, ot_s, dqt_s, dk_s, dv_s,
    pb_out, po, lc, sx, lx, uo, ub, lz, lp, cs, l0, l1, l2, l3,
    lw, r_a, r_b, r_c, s_ab, s_c, rr_c, rr_x, rr_z, rs_c, rs_x, rs_z, r_p, s_p, r_k, s_k, r_l, s_l,
):
    p = lax.axis_index("phase")
    y = lax.axis_index("dp")
    m = lax.axis_index("mp")
    x, z, c = m // 8, (m // 2) % 4, m % 2
    ring_at = p * 4 + z

    sib = (p, y, x * 8 + z * 2 + (1 - c))

    def dev_x(d):
        return (p, y, ((x + d) % 4) * 8 + z * 2 + c)

    def dev_z(zz):
        return (p, y, x * 8 + zz * 2 + c)

    def dev_ring(d):
        at = (ring_at + d + 12) % 12
        return (at // 4, y, x * 8 + (at % 4) * 2 + c)

    def dev_y(d):
        return (p, (y + d) % 8, m)

    def zx(v):
        return (z, z + 1 - 2 * (z % 2), (z + 2) % 4, 3 - z)[v]

    def send(src, dst, ss, rs, dev):
        pltpu.make_async_remote_copy(
            src_ref=src, dst_ref=dst, send_sem=ss, recv_sem=rs, device_id=dev, device_id_type=MESH
        ).start()

    def wait(ref, sem):
        pltpu.make_async_copy(ref, ref, sem).wait()

    loads = [pltpu.make_async_copy(src, g.at[a, c, x, z], lw.at[a]) for a, src in ((M, mem_in), (S, st_in), (T, tg_in))]
    loads.append(pltpu.make_async_copy(wo_in, wo, lw.at[3]))
    for i, (src, dst) in enumerate(((wk_in, wk), (wv_in, wv), (wq_in, wq))):
        for h in range(2):
            loads.append(pltpu.make_async_copy(src.at[:, h], dst.at[h], lw.at[4 + 2 * i + h]))
    ids = [pltpu.make_async_copy(src, dst, lw.at[10 + i]) for i, (src, dst) in enumerate(((src_in, src_ref), (tgt_in, tgt_ref)))]
    for load in loads + ids:
        load.start()

    barrier = pltpu.get_barrier_semaphore()
    greeted = [sib] + [dev_x(d) for d in (1, 2, 3)] + [dev_y(d) for d in range(1, 8)]
    greeted += [dev_ring(d) for d in (-4, -3, -2, -1, 1, 2, 3, 4)]
    for dev in greeted:
        pl.semaphore_signal(barrier, inc=1, device_id=dev, device_id_type=MESH)

    count = cnt_ref[0]
    cs[y] = jnp.full((8, 128), count.astype(F32))
    for load in loads[:3]:
        load.wait()
    pl.semaphore_wait(barrier, len(greeted))

    d2 = 2 - 4 * c

    def blk(a, zz):
        return g.at[a, c, x, zz]

    def to_x(a, zz):
        for d in (2, 1, 3):
            send(blk(a, zz), blk(a, zz), s_ab.at[a], r_b.at[a, d - 1], dev_x(d))

    def to_z(a):
        for v in (3, 2, 1):
            send(blk(a, z), blk(a, z), s_ab.at[a], r_a.at[a, v - 1], dev_z(zx(v)))

    def to_sib(a, d):
        part = g.at[a, c, (x - d + 4) % 4]
        send(part, part, s_c.at[a], r_c.at[a, d], sib)

    def put(a, half, d):
        xx = (x - d + 4) % 4
        rows = g[a, half, xx].reshape(128, TOK)
        if a == T:
            lane = lax.broadcasted_iota(jnp.int32, (128, TOK), 1)
            rows = jnp.where(lane < count, rows.astype(F32), 0.0).astype(BF)
        col = pl.multiple_of(half * 512 + xx * 128, 128)
        xt[a, :, pl.ds(col, 128)] = jnp.transpose(rows)

    rings = ((2, (z + 2) % 4, dev_ring(d2)), (0, (z + 3) % 4, dev_ring(1)), (1, (z + 1) % 4, dev_ring(-1)))

    def to_ring(xx):
        part = g.at[M, c, xx, z]
        for slot, _, dev in rings:
            send(part, part, s_ab.at[M], r_a.at[M, slot], dev)

    def to_sib_m(key, zz):
        part = g.at[M, c, :, zz]
        send(part, part, s_c.at[M], r_c.at[M, key], sib)

    to_x(M, z)
    to_z(S)
    to_ring(x)
    to_x(S, z)
    to_z(T)
    for d in range(1, 8):
        send(cs.at[y], cs.at[y], s_k.at[0], r_k.at[0], dev_y(d))

    for load in ids:
        load.wait()
    src_col = jnp.transpose(jnp.broadcast_to(src_ref[...].astype(F32), (TOK, TOK)))
    bias[...] = jnp.where(src_col == tgt_ref[...].astype(F32), 0.0, NEG)
    loads[3].wait()
    for b in range(8):
        part = jnp.transpose(wo[:, b * 128 : (b + 1) * 128])
        for i in range(4):
            at = b * 4 + i
            wot[at % 2, at // 2] = part[i * 32 : (i + 1) * 32]

    for d in (1, 3, 2):
        xx = (x - d + 4) % 4
        wait(g.at[M, c, xx, z], r_b.at[M, d - 1])
        to_ring(xx)
    to_sib_m(3, z)
    for a in (S, T):
        if a == T:
            to_x(a, z)
        for v in (1, 2, 3):
            wait(blk(a, zx(v)), r_a.at[a, v - 1])
            to_x(a, zx(v))
        to_sib(a, 0)
    put(S, c, 0)

    def arrive_m():
        for slot, zz, _ in (rings[1], rings[2], rings[0]):
            wait(g.at[M, c, :, zz], r_a.at[M, slot])
            to_sib_m(slot, zz)
        for d in range(4):
            put(M, c, d)
        for key, zz in ((3, z), (0, (z + 3) % 4), (1, (z + 1) % 4), (2, (z + 2) % 4)):
            wait(g.at[M, 1 - c, :, zz], r_c.at[M, key])
        for d in range(4):
            put(M, 1 - c, d)

    def arrive(a):
        for d in (1, 3, 2):
            wait(g.at[a, c, (x - d + 4) % 4], r_b.at[a, d - 1])
            to_sib(a, d)
            put(a, c, d)

    def arrive_sib(a):
        for d in (0, 1, 3, 2):
            wait(g.at[a, 1 - c, (x - d + 4) % 4], r_c.at[a, d])
            put(a, 1 - c, d)

    for load in loads[4:]:
        load.wait()
    arrive(S)
    arrive_sib(S)
    q_s[...] = nn(xt[S], wq[...].reshape(1024, 512)).astype(BF)
    arrive_m()
    k_s[...] = nn(xt[M], wk[...].reshape(1024, 512)).astype(BF)
    v_s[...] = nn(xt[M], wv[...].reshape(1024, 512)).astype(BF)
    kt_s[...] = jnp.transpose(k_s[...])
    vt_s[...] = jnp.transpose(v_s[...])

    def head(h):
        return slice(h * HEAD, (h + 1) * HEAD)

    for h in range(HEADS):
        scores = nt(k_s[:, head(h)], q_s[:, head(h)]) + bias[...]
        top = jnp.max(scores, axis=0, keepdims=True)
        e = jnp.exp(scores - top)
        probs = e * (1.0 / jnp.sum(e, axis=0, keepdims=True))
        low = probs.astype(BF)
        p_s[h] = probs
        pb_s[h] = low
        ot_s[head(h), :] = nn(vt_s[head(h), :], low).astype(BF)
        if h == 1:
            put(T, c, 0)
            arrive(T)

    along_z = [(zx(v), v - 1, dev_z(zx(v))) for v in (3, 2, 1)] + [(z, 3, None)]
    along_ring = [((z + 2) % 4, 2, dev_ring(-d2)), ((z + 1) % 4, 0, dev_ring(1)), ((z + 3) % 4, 1, dev_ring(-1))]
    along_x = [((x + d) % 4, d - 1, dev_x(d)) for d in (2, 1, 3)] + [(x, 3, None)]

    def chunk(i, buf, at):
        return buf.at[i, at] if i == GM else buf.at[i, :, at]

    def sum_start(i, part):
        pb_out[i] = part(1 - c).astype(BF).reshape(4, 4, 32, TOK)
        for at, key, _ in along_x if i == GM else along_z:
            send(chunk(i, pb_out, at), chunk(i, lc, at), rs_c.at[i], rr_c.at[i, key], sib)
        po[i] = part(c).reshape(4, 4, 32, TOK)

    def sum_first(i):
        for at, key, _ in along_x if i == GM else along_z:
            wait(chunk(i, lc, at), rr_c.at[i, key])
            if i == GM:
                total = po[i, at] + lc[i, at].astype(F32)
                po[i, at] = total
                sx[i, at] = total.astype(BF)
                for zz, slot, dev in along_ring:
                    send(sx.at[i, at, zz], lx.at[i, at, slot], rs_x.at[i], rr_x.at[i, key], dev)
            else:
                total = po[i, :, at] + lc[i, :, at].astype(F32)
                po[i, :, at] = total
                sx[i, :, at] = total.astype(BF)
                for xx, slot, dev in along_x[:3]:
                    send(sx.at[i, xx, at], lx.at[i, at, slot], rs_x.at[i], rr_x.at[i, key], dev)

    def sum_second(i):
        for at, key, dev in along_x if i == GM else along_z:
            wait(lx.at[i, at], rr_x.at[i, key])
            got = lx[i, at].astype(F32)
            total = (po[i, at, z] if i == GM else po[i, x, at]) + got[0] + got[1] + got[2]
            if dev is None:
                uo[i] = total
            else:
                ub[i, at] = total.astype(BF)
                send(ub.at[i, at], lz.at[i, key], rs_z.at[i], rr_z.at[i, key], dev)

    def sum_end(i):
        for key in range(3):
            wait(lz.at[i, key], rr_z.at[i, key])
        got = lz[i].astype(F32)
        return uo[i] + got[0] + got[1] + got[2]

    sum_start(OUT, lambda half: nn(wot[half].reshape(512, 512), ot_s[...]))
    arrive_sib(T)
    do_s[...] = nn(xt[T], wot[...].reshape(1024, 512)).astype(BF)
    sum_first(OUT)

    inner_all = jnp.zeros((1, TOK), F32)
    for h in range(HEADS):
        dprob = nt(v_s[:, head(h)], do_s[:, head(h)])
        probs = p_s[h]
        inner = jnp.sum(probs * dprob, axis=0, keepdims=True)
        inner_all += inner
        ds_s[h] = (probs * (dprob - inner)).astype(BF)
    row = lax.broadcasted_iota(jnp.int32, (8, 128), 0)
    folded = jnp.broadcast_to(inner_all[:, :128] + inner_all[:, 128:], (8, 128))
    l3[y] = jnp.where(row == 0, folded, 0.0)
    for d in range(1, 8):
        send(l3.at[y], l3.at[y], s_l.at[3], r_l.at[3], dev_y(d))
    for h in range(HEADS):
        dk_s[:, head(h)] = nn(ds_s[h], q_s[:, head(h)]).astype(BF)
        dv_s[:, head(h)] = nn(pb_s[h], do_s[:, head(h)]).astype(BF)

    def part_gm(half):
        return nt(wk[half].reshape(512, 512), dk_s[...]) + nt(wv[half].reshape(512, 512), dv_s[...])

    sum_start(GM, part_gm)
    for h in range(HEADS):
        dqt_s[head(h), :] = nn(kt_s[head(h), :], ds_s[h]).astype(BF)
    sum_first(GM)
    sum_start(GX, lambda half: nn(wq[half].reshape(512, 512), dqt_s[...]))
    sum_first(GX)
    sum_second(OUT)
    wait(l3.at[pl.ds(0, 7)], r_l.at[3])
    l0[c] = jnp.sum(l3[...], axis=0)
    send(l0.at[c], l0.at[c], s_l.at[0], r_l.at[0], sib)
    sum_second(GM)
    wait(l0.at[1 - c], r_l.at[0])
    l1[x] = l0[0] + l0[1]
    for d in (1, 2, 3):
        send(l1.at[x], l1.at[x], s_l.at[1], r_l.at[1], dev_x(d))
    lp[p] = sum_end(GM).astype(BF)
    for d in (-4, 4):
        send(lp.at[p], lp.at[p], s_p.at[0], r_p.at[0], dev_ring(d))
    wait(l1.at[pl.ds(0, 3)], r_l.at[1])
    l2[z] = (l1[0] + l1[1]) + (l1[2] + l1[3])
    for v in (1, 2, 3):
        send(l2.at[z], l2.at[z], s_l.at[2], r_l.at[2], dev_z(zx(v)))
    sum_second(GX)
    out_o[...] = sum_end(OUT).astype(BF)
    wait(cs.at[pl.ds(0, 7)], r_k.at[0])
    tot = jnp.sum(cs[...], axis=0)
    tot_row = tot[0:1, 0:1]
    tot_all = jnp.broadcast_to(tot_row, (32, TOK))
    wait(l2.at[pl.ds(0, 3)], r_l.at[2])
    loss = jnp.sum((l2[0] + l2[1]) + (l2[2] + l2[3]), keepdims=True)
    loss_o[...] = jnp.broadcast_to(loss / tot_row, (8, 128))
    gx_o[...] = (sum_end(GX) / tot_all).astype(BF)
    wait(lp.at[pl.ds(0, 2)], r_p.at[0])
    got = lp[...].astype(F32)
    gm_o[...] = ((got[0] + got[1] + got[2]) / tot_all).astype(BF)

    for a in range(3):
        wait(k_s.at[pl.ds(0, 240)], s_ab.at[a])
        wait(g.at[a, 0], s_c.at[a])
        wait(pb_out.at[a], rs_c.at[a])
        wait(sx.at[a, pl.ds(0, 3)], rs_x.at[a])
        wait(ub.at[a, pl.ds(0, 3)], rs_z.at[a])
    wait(lp.at[pl.ds(0, 2)], s_p.at[0])
    wait(cs.at[pl.ds(0, 7)], s_k.at[0])
    wait(l0.at[0], s_l.at[0])
    wait(l1.at[pl.ds(0, 3)], s_l.at[1])
    wait(l2.at[pl.ds(0, 3)], s_l.at[2])
    wait(l3.at[pl.ds(0, 7)], s_l.at[3])


def place_kernel(out_i, gx_i, gm_i, loss_i, out_o, gx_o, gm_o, loss_o):
    out_o[...] = out_i[...]
    gx_o[...] = gx_i[...]
    gm_o[...] = gm_i[...]
    loss_o[0] = loss_i[0, 0]


def local(memory, states, targets, w_query, w_key, w_value, w_out, src_ids, tgt_ids, counts):
    vmem = pl.BlockSpec(memory_space=pltpu.VMEM)
    smem = pl.BlockSpec(memory_space=pltpu.SMEM)
    hbm = pl.BlockSpec(memory_space=pl.ANY)
    dma = pltpu.SemaphoreType.DMA
    block = jax.ShapeDtypeStruct((32, TOK), BF)
    split = (16, 2, 32, 512)

    def v(shape, dtype=BF):
        return pltpu.VMEM(shape, dtype)

    results = pl.pallas_call(
        main_kernel,
        out_shape=(block, block, block, jax.ShapeDtypeStruct((8, 128), F32)),
        in_specs=[hbm] * 9 + [smem],
        out_specs=[vmem] * 4,
        scratch_shapes=[
            v((2, 16, 32, 512)), v((2, 16, 32, 512)), v((2, 16, 32, 512)), v((512, 1024)), v((2, 16, 32, 512)),
            v((3, 2, 4, 4, 32, TOK)), v((3, TOK, 1024)), v((TOK, TOK), F32),
            v((1, TOK), jnp.int32), v((1, TOK), jnp.int32),
            v((TOK, 512)), v((TOK, 512)), v((TOK, 512)), v((512, TOK)), v((512, TOK)), v((TOK, 512)),
            v((HEADS, TOK, TOK), F32), v((HEADS, TOK, TOK)), v((HEADS, TOK, TOK)), v((512, TOK)), v((512, TOK)), v((TOK, 512)), v((TOK, 512)),
            v((3, 4, 4, 32, TOK)), v((3, 4, 4, 32, TOK), F32), v((3, 4, 4, 32, TOK)), v((3, 4, 4, 32, TOK)),
            v((3, 4, 3, 32, TOK)), v((3, 32, TOK), F32), v((3, 4, 32, TOK)), v((3, 3, 32, TOK)), v((3, 32, TOK)),
            v((8, 8, 128), F32), v((2, 8, 128), F32), v((4, 8, 128), F32), v((4, 8, 128), F32), v((8, 8, 128), F32),
            dma((12,)), dma((3, 3)), dma((3, 3)), dma((3, 4)), dma((3,)), dma((3,)),
            dma((3, 4)), dma((3, 4)), dma((3, 3)), dma((3,)), dma((3,)), dma((3,)),
            dma((1,)), dma((1,)), dma((1,)), dma((1,)), dma((4,)), dma((4,)),
        ],
        compiler_params=pltpu.CompilerParams(
            collective_id=0, has_side_effects=True, vmem_limit_bytes=62 * 1024 * 1024
        ),
        name="cross_attention",
    )(
        memory[0].T, states[0, 0].T, targets[0, 0].T,
        w_query.reshape(split), w_key.reshape(split), w_value.reshape(split), w_out[0],
        src_ids, tgt_ids, counts,
    )
    out, gx, gm, loss = pl.pallas_call(
        place_kernel,
        out_shape=(block, block, block, jax.ShapeDtypeStruct((1,), F32)),
        in_specs=[vmem, vmem, vmem, smem],
        out_specs=[vmem, vmem, vmem, smem],
        name="place_outputs",
    )(*results)
    return out.T[None, None], loss, gx.T[None, None], gm.T[None]


def solution(mesh):
    placed = (
        P("dp", None, "mp"),
        P("phase", "dp", None, "mp"),
        P("phase", "dp", None, "mp"),
        P("phase", None, "mp"),
        P("phase", None, "mp"),
        P("phase", None, "mp"),
        P("phase", "mp", None),
        P("dp", None),
        P("dp", None),
        P("dp"),
    )
    return jax.shard_map(
        local,
        mesh=mesh,
        in_specs=placed,
        out_specs=(
            P("phase", "dp", None, "mp"),
            P("phase"),
            P("phase", "dp", None, "mp"),
            P("dp", None, "mp"),
        ),
        check_vma=False,
    )
```

```python
import jax
import jax.numpy as jnp
from jax import lax
from jax.experimental import pallas as pl
from jax.experimental.pallas import tpu as pltpu
from jax.sharding import PartitionSpec as P


BF = jnp.bfloat16
F32 = jnp.float32
MESH = pl.DeviceIdType.MESH
HEADS = 4
HEAD = 128
TOK = 256
NEG = -1e30
M, S, T = 0, 1, 2
OUT, GM, GX = 0, 1, 2


def nn(a, b):
    return lax.dot_general(a, b, (((1,), (0,)), ((), ())), preferred_element_type=F32)


def nt(a, b):
    return lax.dot_general(a, b, (((1,), (1,)), ((), ())), preferred_element_type=F32)


def main_kernel(
    mem_in, st_in, tg_in, wq_in, wk_in, wv_in, wo_in, src_in, tgt_in, cnt_ref,
    out_o, gx_o, gm_o, loss_o,
    wq, wk, wv, wo, wot, g, xt, bias, src_ref, tgt_ref,
    q_s, k_s, v_s, kt_s, vt_s, do_s, p_s, pb_s, ds_s, ot_s, dqt_s, dk_s, dv_s,
    pb_out, po, lc, sx, lx, uo, ub, lz, lp, cs, l0, l1, l2, l3,
    lw, r_a, r_b, r_c, s_ab, s_c, rr_c, rr_x, rr_z, rs_c, rs_x, rs_z, r_p, s_p, r_k, s_k, r_l, s_l,
):
    p = lax.axis_index("phase")
    y = lax.axis_index("dp")
    m = lax.axis_index("mp")
    x, z, c = m // 8, (m // 2) % 4, m % 2
    ring_at = p * 4 + z

    sib = (p, y, x * 8 + z * 2 + (1 - c))

    def dev_x(d):
        return (p, y, ((x + d) % 4) * 8 + z * 2 + c)

    def dev_z(zz):
        return (p, y, x * 8 + zz * 2 + c)

    def dev_ring(d):
        at = (ring_at + d + 12) % 12
        return (at // 4, y, x * 8 + (at % 4) * 2 + c)

    def dev_y(d):
        return (p, (y + d) % 8, m)

    def zx(v):
        return (z, z + 1 - 2 * (z % 2), (z + 2) % 4, 3 - z)[v]

    def send(src, dst, ss, rs, dev):
        pltpu.make_async_remote_copy(
            src_ref=src, dst_ref=dst, send_sem=ss, recv_sem=rs, device_id=dev, device_id_type=MESH
        ).start()

    def wait(ref, sem):
        pltpu.make_async_copy(ref, ref, sem).wait()

    loads = [pltpu.make_async_copy(src, g.at[a, c, x, z], lw.at[a]) for a, src in ((M, mem_in), (S, st_in), (T, tg_in))]
    loads.append(pltpu.make_async_copy(wo_in, wo, lw.at[3]))
    for i, (src, dst) in enumerate(((wk_in, wk), (wv_in, wv), (wq_in, wq))):
        for h in range(2):
            loads.append(pltpu.make_async_copy(src.at[:, h], dst.at[h], lw.at[4 + 2 * i + h]))
    ids = [pltpu.make_async_copy(src, dst, lw.at[10 + i]) for i, (src, dst) in enumerate(((src_in, src_ref), (tgt_in, tgt_ref)))]
    for load in loads + ids:
        load.start()

    barrier = pltpu.get_barrier_semaphore()
    greeted = [sib] + [dev_x(d) for d in (1, 2, 3)] + [dev_y(d) for d in range(1, 8)]
    greeted += [dev_ring(d) for d in (-4, -3, -2, -1, 1, 2, 3, 4)]
    for dev in greeted:
        pl.semaphore_signal(barrier, inc=1, device_id=dev, device_id_type=MESH)

    count = cnt_ref[0]
    cs[y] = jnp.full((8, 128), count.astype(F32))
    for load in loads[:3]:
        load.wait()
    pl.semaphore_wait(barrier, len(greeted))

    d2 = 2 - 4 * c

    def blk(a, zz):
        return g.at[a, c, x, zz]

    def to_x(a, zz):
        for d in (2, 1, 3):
            send(blk(a, zz), blk(a, zz), s_ab.at[a], r_b.at[a, d - 1], dev_x(d))

    def to_z(a):
        for v in (3, 2, 1):
            send(blk(a, z), blk(a, z), s_ab.at[a], r_a.at[a, v - 1], dev_z(zx(v)))

    def to_sib(a, d):
        part = g.at[a, c, (x - d + 4) % 4]
        send(part, part, s_c.at[a], r_c.at[a, d], sib)

    def put(a, half, d):
        xx = (x - d + 4) % 4
        rows = g[a, half, xx].reshape(128, TOK)
        if a == T:
            lane = lax.broadcasted_iota(jnp.int32, (128, TOK), 1)
            rows = jnp.where(lane < count, rows.astype(F32), 0.0).astype(BF)
        col = pl.multiple_of(half * 512 + xx * 128, 128)
        xt[a, :, pl.ds(col, 128)] = jnp.transpose(rows)

    rings = ((2, (z + 2) % 4, dev_ring(d2)), (0, (z + 3) % 4, dev_ring(1)), (1, (z + 1) % 4, dev_ring(-1)))

    def to_ring(xx):
        part = g.at[M, c, xx, z]
        for slot, _, dev in rings:
            send(part, part, s_ab.at[M], r_a.at[M, slot], dev)

    def to_sib_m(key, zz):
        part = g.at[M, c, :, zz]
        send(part, part, s_c.at[M], r_c.at[M, key], sib)

    to_x(M, z)
    to_z(S)
    to_ring(x)
    to_x(S, z)
    to_z(T)
    for d in range(1, 8):
        send(cs.at[y], cs.at[y], s_k.at[0], r_k.at[0], dev_y(d))

    for load in ids:
        load.wait()
    src_col = jnp.transpose(jnp.broadcast_to(src_ref[...].astype(F32), (TOK, TOK)))
    bias[...] = jnp.where(src_col == tgt_ref[...].astype(F32), 0.0, NEG)
    loads[3].wait()
    for b in range(8):
        part = jnp.transpose(wo[:, b * 128 : (b + 1) * 128])
        for i in range(4):
            at = b * 4 + i
            wot[at % 2, at // 2] = part[i * 32 : (i + 1) * 32]

    for d in (1, 3, 2):
        xx = (x - d + 4) % 4
        wait(g.at[M, c, xx, z], r_b.at[M, d - 1])
        to_ring(xx)
    to_sib_m(3, z)
    for a in (S, T):
        if a == T:
            to_x(a, z)
        for v in (1, 2, 3):
            wait(blk(a, zx(v)), r_a.at[a, v - 1])
            to_x(a, zx(v))
        to_sib(a, 0)
    put(S, c, 0)

    def arrive_m():
        for slot, zz, _ in (rings[1], rings[2], rings[0]):
            wait(g.at[M, c, :, zz], r_a.at[M, slot])
            to_sib_m(slot, zz)
        for d in range(4):
            put(M, c, d)
        for key, zz in ((3, z), (0, (z + 3) % 4), (1, (z + 1) % 4), (2, (z + 2) % 4)):
            wait(g.at[M, 1 - c, :, zz], r_c.at[M, key])
        for d in range(4):
            put(M, 1 - c, d)

    def arrive(a):
        for d in (1, 3, 2):
            wait(g.at[a, c, (x - d + 4) % 4], r_b.at[a, d - 1])
            to_sib(a, d)
            put(a, c, d)

    def arrive_sib(a):
        for d in (0, 1, 3, 2):
            wait(g.at[a, 1 - c, (x - d + 4) % 4], r_c.at[a, d])
            put(a, 1 - c, d)

    for load in loads[4:]:
        load.wait()
    arrive(S)
    arrive_sib(S)
    q_s[...] = nn(xt[S], wq[...].reshape(1024, 512)).astype(BF)
    arrive_m()
    k_s[...] = nn(xt[M], wk[...].reshape(1024, 512)).astype(BF)
    v_s[...] = nn(xt[M], wv[...].reshape(1024, 512)).astype(BF)
    put(T, c, 0)
    arrive(T)
    kt_s[...] = jnp.transpose(k_s[...])
    vt_s[...] = jnp.transpose(v_s[...])

    def head(h):
        return slice(h * HEAD, (h + 1) * HEAD)

    for h in range(HEADS):
        scores = nt(k_s[:, head(h)], q_s[:, head(h)]) + bias[...]
        top = jnp.max(scores, axis=0, keepdims=True)
        e = jnp.exp(scores - top)
        probs = e * (1.0 / jnp.sum(e, axis=0, keepdims=True))
        low = probs.astype(BF)
        p_s[h] = probs
        pb_s[h] = low
        ot_s[head(h), :] = nn(vt_s[head(h), :], low).astype(BF)

    along_z = [(zx(v), v - 1, dev_z(zx(v))) for v in (3, 2, 1)] + [(z, 3, None)]
    along_ring = [((z + 2) % 4, 2, dev_ring(-d2)), ((z + 1) % 4, 0, dev_ring(1)), ((z + 3) % 4, 1, dev_ring(-1))]
    along_x = [((x + d) % 4, d - 1, dev_x(d)) for d in (2, 1, 3)] + [(x, 3, None)]

    def chunk(i, buf, at):
        return buf.at[i, at] if i == GM else buf.at[i, :, at]

    def sum_start(i, part):
        pb_out[i] = part(1 - c).astype(BF).reshape(4, 4, 32, TOK)
        for at, key, _ in along_x if i == GM else along_z:
            send(chunk(i, pb_out, at), chunk(i, lc, at), rs_c.at[i], rr_c.at[i, key], sib)
        po[i] = part(c).reshape(4, 4, 32, TOK)

    def sum_first(i):
        for at, key, _ in along_x if i == GM else along_z:
            wait(chunk(i, lc, at), rr_c.at[i, key])
            if i == GM:
                total = po[i, at] + lc[i, at].astype(F32)
                po[i, at] = total
                sx[i, at] = total.astype(BF)
                for zz, slot, dev in along_ring:
                    send(sx.at[i, at, zz], lx.at[i, at, slot], rs_x.at[i], rr_x.at[i, key], dev)
            else:
                total = po[i, :, at] + lc[i, :, at].astype(F32)
                po[i, :, at] = total
                sx[i, :, at] = total.astype(BF)
                for xx, slot, dev in along_x[:3]:
                    send(sx.at[i, xx, at], lx.at[i, at, slot], rs_x.at[i], rr_x.at[i, key], dev)

    def sum_second(i):
        for at, key, dev in along_x if i == GM else along_z:
            wait(lx.at[i, at], rr_x.at[i, key])
            got = lx[i, at].astype(F32)
            total = (po[i, at, z] if i == GM else po[i, x, at]) + got[0] + got[1] + got[2]
            if dev is None:
                uo[i] = total
            else:
                ub[i, at] = total.astype(BF)
                send(ub.at[i, at], lz.at[i, key], rs_z.at[i], rr_z.at[i, key], dev)

    def sum_end(i):
        for key in range(3):
            wait(lz.at[i, key], rr_z.at[i, key])
        got = lz[i].astype(F32)
        return uo[i] + got[0] + got[1] + got[2]

    sum_start(OUT, lambda half: nn(wot[half].reshape(512, 512), ot_s[...]))
    arrive_sib(T)
    do_s[...] = nn(xt[T], wot[...].reshape(1024, 512)).astype(BF)
    sum_first(OUT)

    inner_all = jnp.zeros((1, TOK), F32)
    for h in range(HEADS):
        dprob = nt(v_s[:, head(h)], do_s[:, head(h)])
        probs = p_s[h]
        inner = jnp.sum(probs * dprob, axis=0, keepdims=True)
        inner_all += inner
        ds_s[h] = (probs * (dprob - inner)).astype(BF)
    row = lax.broadcasted_iota(jnp.int32, (8, 128), 0)
    folded = jnp.broadcast_to(inner_all[:, :128] + inner_all[:, 128:], (8, 128))
    l3[y] = jnp.where(row == 0, folded, 0.0)
    for d in range(1, 8):
        send(l3.at[y], l3.at[y], s_l.at[3], r_l.at[3], dev_y(d))
    for h in range(HEADS):
        dk_s[:, head(h)] = nn(ds_s[h], q_s[:, head(h)]).astype(BF)
        dv_s[:, head(h)] = nn(pb_s[h], do_s[:, head(h)]).astype(BF)

    def part_gm(half):
        return nt(wk[half].reshape(512, 512), dk_s[...]) + nt(wv[half].reshape(512, 512), dv_s[...])

    sum_start(GM, part_gm)
    for h in range(HEADS):
        dqt_s[head(h), :] = nn(kt_s[head(h), :], ds_s[h]).astype(BF)
    sum_first(GM)
    sum_start(GX, lambda half: nn(wq[half].reshape(512, 512), dqt_s[...]))
    sum_first(GX)
    sum_second(OUT)
    wait(l3.at[pl.ds(0, 7)], r_l.at[3])
    l0[c] = jnp.sum(l3[...], axis=0)
    send(l0.at[c], l0.at[c], s_l.at[0], r_l.at[0], sib)
    sum_second(GM)
    wait(l0.at[1 - c], r_l.at[0])
    l1[x] = l0[0] + l0[1]
    for d in (1, 2, 3):
        send(l1.at[x], l1.at[x], s_l.at[1], r_l.at[1], dev_x(d))
    lp[p] = sum_end(GM).astype(BF)
    for d in (-4, 4):
        send(lp.at[p], lp.at[p], s_p.at[0], r_p.at[0], dev_ring(d))
    wait(l1.at[pl.ds(0, 3)], r_l.at[1])
    l2[z] = (l1[0] + l1[1]) + (l1[2] + l1[3])
    for v in (1, 2, 3):
        send(l2.at[z], l2.at[z], s_l.at[2], r_l.at[2], dev_z(zx(v)))
    sum_second(GX)
    out_o[...] = sum_end(OUT).astype(BF)
    wait(cs.at[pl.ds(0, 7)], r_k.at[0])
    tot = jnp.sum(cs[...], axis=0)
    tot_row = tot[0:1, 0:1]
    tot_all = jnp.broadcast_to(tot_row, (32, TOK))
    wait(l2.at[pl.ds(0, 3)], r_l.at[2])
    loss = jnp.sum((l2[0] + l2[1]) + (l2[2] + l2[3]), keepdims=True)
    loss_o[...] = jnp.broadcast_to(loss / tot_row, (8, 128))
    gx_o[...] = (sum_end(GX) / tot_all).astype(BF)
    wait(lp.at[pl.ds(0, 2)], r_p.at[0])
    got = lp[...].astype(F32)
    gm_o[...] = ((got[0] + got[1] + got[2]) / tot_all).astype(BF)

    for a in range(3):
        wait(k_s.at[pl.ds(0, 240)], s_ab.at[a])
        wait(g.at[a, 0], s_c.at[a])
        wait(pb_out.at[a], rs_c.at[a])
        wait(sx.at[a, pl.ds(0, 3)], rs_x.at[a])
        wait(ub.at[a, pl.ds(0, 3)], rs_z.at[a])
    wait(lp.at[pl.ds(0, 2)], s_p.at[0])
    wait(cs.at[pl.ds(0, 7)], s_k.at[0])
    wait(l0.at[0], s_l.at[0])
    wait(l1.at[pl.ds(0, 3)], s_l.at[1])
    wait(l2.at[pl.ds(0, 3)], s_l.at[2])
    wait(l3.at[pl.ds(0, 7)], s_l.at[3])


def place_kernel(out_i, gx_i, gm_i, loss_i, out_o, gx_o, gm_o, loss_o):
    out_o[...] = out_i[...]
    gx_o[...] = gx_i[...]
    gm_o[...] = gm_i[...]
    loss_o[0] = loss_i[0, 0]


def local(memory, states, targets, w_query, w_key, w_value, w_out, src_ids, tgt_ids, counts):
    vmem = pl.BlockSpec(memory_space=pltpu.VMEM)
    smem = pl.BlockSpec(memory_space=pltpu.SMEM)
    hbm = pl.BlockSpec(memory_space=pl.ANY)
    dma = pltpu.SemaphoreType.DMA
    block = jax.ShapeDtypeStruct((32, TOK), BF)
    split = (16, 2, 32, 512)

    def v(shape, dtype=BF):
        return pltpu.VMEM(shape, dtype)

    results = pl.pallas_call(
        main_kernel,
        out_shape=(block, block, block, jax.ShapeDtypeStruct((8, 128), F32)),
        in_specs=[hbm] * 9 + [smem],
        out_specs=[vmem] * 4,
        scratch_shapes=[
            v((2, 16, 32, 512)), v((2, 16, 32, 512)), v((2, 16, 32, 512)), v((512, 1024)), v((2, 16, 32, 512)),
            v((3, 2, 4, 4, 32, TOK)), v((3, TOK, 1024)), v((TOK, TOK), F32),
            v((1, TOK), jnp.int32), v((1, TOK), jnp.int32),
            v((TOK, 512)), v((TOK, 512)), v((TOK, 512)), v((512, TOK)), v((512, TOK)), v((TOK, 512)),
            v((HEADS, TOK, TOK), F32), v((HEADS, TOK, TOK)), v((HEADS, TOK, TOK)), v((512, TOK)), v((512, TOK)), v((TOK, 512)), v((TOK, 512)),
            v((3, 4, 4, 32, TOK)), v((3, 4, 4, 32, TOK), F32), v((3, 4, 4, 32, TOK)), v((3, 4, 4, 32, TOK)),
            v((3, 4, 3, 32, TOK)), v((3, 32, TOK), F32), v((3, 4, 32, TOK)), v((3, 3, 32, TOK)), v((3, 32, TOK)),
            v((8, 8, 128), F32), v((2, 8, 128), F32), v((4, 8, 128), F32), v((4, 8, 128), F32), v((8, 8, 128), F32),
            dma((12,)), dma((3, 3)), dma((3, 3)), dma((3, 4)), dma((3,)), dma((3,)),
            dma((3, 4)), dma((3, 4)), dma((3, 3)), dma((3,)), dma((3,)), dma((3,)),
            dma((1,)), dma((1,)), dma((1,)), dma((1,)), dma((4,)), dma((4,)),
        ],
        compiler_params=pltpu.CompilerParams(
            collective_id=0, has_side_effects=True, vmem_limit_bytes=62 * 1024 * 1024
        ),
        name="cross_attention",
    )(
        memory[0].T, states[0, 0].T, targets[0, 0].T,
        w_query.reshape(split), w_key.reshape(split), w_value.reshape(split), w_out[0],
        src_ids, tgt_ids, counts,
    )
    out, gx, gm, loss = pl.pallas_call(
        place_kernel,
        out_shape=(block, block, block, jax.ShapeDtypeStruct((1,), F32)),
        in_specs=[vmem, vmem, vmem, smem],
        out_specs=[vmem, vmem, vmem, smem],
        name="place_outputs",
    )(*results)
    return out.T[None, None], loss, gx.T[None, None], gm.T[None]


def solution(mesh):
    placed = (
        P("dp", None, "mp"),
        P("phase", "dp", None, "mp"),
        P("phase", "dp", None, "mp"),
        P("phase", None, "mp"),
        P("phase", None, "mp"),
        P("phase", None, "mp"),
        P("phase", "mp", None),
        P("dp", None),
        P("dp", None),
        P("dp"),
    )
    return jax.shard_map(
        local,
        mesh=mesh,
        in_specs=placed,
        out_specs=(
            P("phase", "dp", None, "mp"),
            P("phase"),
            P("phase", "dp", None, "mp"),
            P("dp", None, "mp"),
        ),
        check_vma=False,
    )
```
